128 devices in a mesh: row: 8 (over z, core), col: 16 (over x, y).
Axes of the slice: x: 4, y: 4, z: 4, core: 2. Of those that a mesh axis runs over, the one named last changes fastest.
Arguments:
- inputs: bfloat16 [1024, 12288], P('col', 'row'), may hold values from -6 to 6
- w_in: bfloat16 [12288, 24576], P('row', 'col'), may hold values from -0.0546875 to 0.0546875
- w_out: bfloat16 [24576, 12288], P('col', 'row'), may hold values from -0.0390625 to 0.0390625
- cotangent: bfloat16 [1024, 12288], P('col', 'row'), may hold values from -3 to 3
Outputs:
- output: bfloat16 [1024, 12288], P('col', 'row')
- grad_inputs: bfloat16 [1024, 12288], P('col', 'row')
- grad_w_in: bfloat16 [12288, 24576], P('row', 'col')
- grad_w_out: bfloat16 [24576, 12288], P('col', 'row')
The draws below stay inside these ranges and needn't reach their ends.
All inputs are finite; a program needn't handle non-finite values.
Results may differ from the reference program's by a relative error of at most 0.005.
Values may be sent and summed in bfloat16 or wider, within the bound.
No kernel may reach another device: no remote copies, remote signals or barrier semaphores. Data moves between devices by JAX's collectives and lax.ppermute only.
A program may use at most 128 MiB of HBM per device.

```python
import jax
import jax.numpy as jnp

D = 12288
FF = 24576
TOKENS = 1024


def block_scale(stream_key, shape, shards, smallest, largest):
    def one(position, shards_of):
        draws = jax.random.uniform(jax.random.fold_in(jax.random.fold_in(stream_key, 6), position), (shards_of,), jnp.float32, smallest / len(shards), largest / len(shards))
        return jnp.repeat(jnp.exp(draws), shape[position] // shards_of).reshape((-1,) + (1,) * (len(shape) - position - 1))

    level = one(*shards[0])
    for cut in shards[1:]:
        level = level * one(*cut)
    return level


def scatter_about(key, extent, spread, bound, pieces=(), dtype=jnp.bfloat16):
    entries = jax.random.normal(key, extent, jnp.float32) * spread
    if len(pieces) > 0:
        entries = block_scale(key, extent, pieces, -0.22, 0.18) * entries
    return jnp.clip(entries, min=-bound, max=bound).astype(dtype)


def setup_inputs(seed: int = 0) -> dict:
    arg_keys = jax.random.split(jax.random.key(seed), 5)
    return {
        "inputs": scatter_about(arg_keys[0], (TOKENS, D), 1.0, 6.0, ((0, 16), (1, 8))),
        "w_in": scatter_about(arg_keys[1], (D, FF), D ** -0.5, 0.0546875, ((0, 8), (1, 16))),
        "w_out": scatter_about(arg_keys[2], (FF, D), FF ** -0.5, 0.0390625, ((0, 16), (1, 8))),
        "cotangent": scatter_about(arg_keys[3], (TOKENS, D), 0.5, 3.0, ((0, 16), (1, 8))),
    }


def gelu_form(value):
    return jax.nn.gelu(value, approximate=True)

def gelu_backward(value, grad):
    return jax.vjp(gelu_form, value)[1](grad)[0]

def reference(inputs, w_in, w_out, cotangent):
    hidden = jnp.dot(inputs, w_in, preferred_element_type=jnp.float32)
    activated = gelu_form(hidden).astype(jnp.bfloat16)
    output = jnp.dot(activated, w_out, preferred_element_type=jnp.float32).astype(jnp.bfloat16)
    grad_w_out = jnp.dot(activated.T, cotangent, preferred_element_type=jnp.float32).astype(jnp.bfloat16)
    grad_activated = jnp.dot(cotangent, w_out.T, preferred_element_type=jnp.float32)
    grad_hidden = gelu_backward(hidden, grad_activated).astype(jnp.bfloat16)
    grad_w_in = jnp.dot(inputs.T, grad_hidden, preferred_element_type=jnp.float32).astype(jnp.bfloat16)
    grad_inputs = jnp.dot(grad_hidden, w_in.T, preferred_element_type=jnp.float32).astype(jnp.bfloat16)
    return (output, grad_inputs, grad_w_in, grad_w_out)
```

```python
import functools

import jax
import jax.numpy as jnp
from jax import lax
from jax.experimental import pallas as pl
from jax.experimental.pallas import tpu as pltpu
from jax.sharding import PartitionSpec as P

BF16 = jnp.bfloat16
F32 = jnp.float32
AXES = ("row", "col")
RING = 4
TILE = 256
LIMIT = 40 * 1024 * 1024


def gelu_form(value):
    return jax.nn.gelu(value, approximate=True)


def gelu_backward(value, grad):
    return jax.vjp(gelu_form, value)[1](grad)[0]


def permutation(first=0, second=0, up=0, other=0):
    pairs = []
    for z in range(RING):
        for core in range(2):
            for x in range(RING):
                for y in range(RING):
                    step_x, step_y = (first, second) if core == 0 else (second, first)
                    to_row = ((z + up) % RING) * 2 + (core + other) % 2
                    to_col = ((x + step_x) % RING) * RING + (y + step_y) % RING
                    pairs.append(((z * 2 + core) * 16 + x * RING + y, to_row * 16 + to_col))
    return pairs


def send(block, **where):
    return lax.ppermute(block, AXES, permutation(**where))


def swap(block):
    return send(block, other=1)


def gather_ring(block, axis):
    return [block] + [send(block, **{axis: -step}) for step in range(1, RING)]


def scatter_ring(blocks, axis):
    got = [send(blocks[step], **{axis: step}) for step in range(1, RING)]
    total = blocks[0].astype(F32)
    for block in got:
        total = total + block.astype(F32)
    return total


def cost(rows, depth, columns, moved):
    return pl.CostEstimate(flops=2 * rows * depth * columns, bytes_accessed=moved, transcendentals=0)


def dot(left, right, transposed):
    return lax.dot_general(left, right, (((1,), (1 if transposed else 0,)), ((), ())), preferred_element_type=F32)


def up_kernel(transposed, place, p0, p1, p2, p3, w_own, w_other, h0, h1, h2, h3, own, other, scratch):
    rows = p0.shape[0]
    depth = own.shape[1]

    @pl.when(pl.program_id(0) == 0)
    def _():
        for index, piece in enumerate((p0, p1, p2, p3)):
            own[index * rows : (index + 1) * rows, :] = piece[:, :depth]
            other[index * rows : (index + 1) * rows, :] = piece[:, depth:]

    total = dot(own[...], w_own[...], transposed) + dot(other[...], w_other[...], transposed)
    scratch[...] = total.astype(BF16)
    for index, out in enumerate((h0, h1, h2, h3)):
        start = pl.multiple_of(lax.rem(place[0] + index, RING) * rows, rows)
        out[...] = scratch[pl.ds(start, rows), :]


def project_up(place, pieces, w_own, w_other, transposed):
    rows, width = pieces[0].shape
    depth = width // 2
    columns = w_own.shape[0 if transposed else 1]
    tile = min(TILE, columns)
    whole = pl.BlockSpec((rows, width), lambda n: (0, 0))
    if transposed:
        weight = pl.BlockSpec((tile, depth), lambda n: (n, 0))
    else:
        weight = pl.BlockSpec((depth, tile), lambda n: (0, n))
    kept = pl.BlockSpec((RING * rows, depth), lambda n: (0, 0))
    outs = pl.pallas_call(
        functools.partial(up_kernel, transposed),
        grid=(columns // tile,),
        in_specs=[pl.BlockSpec(memory_space=pltpu.SMEM)] + [whole] * RING + [weight] * 2,
        out_specs=[pl.BlockSpec((rows, tile), lambda n: (0, n))] * RING + [kept] * 2,
        out_shape=[jax.ShapeDtypeStruct((rows, columns), BF16)] * RING
        + [jax.ShapeDtypeStruct((RING * rows, depth), BF16)] * 2,
        scratch_shapes=[pltpu.VMEM((RING * rows, tile), BF16)],
        compiler_params=pltpu.CompilerParams(vmem_limit_bytes=LIMIT),
        cost_estimate=cost(RING * rows, width, columns, 2 * (width * columns + 2 * RING * rows * width)),
    )(place, *pieces, w_own, w_other)
    return outs[:RING], outs[RING], outs[RING + 1]


def down_kernel(transposed, place, p0, p1, p2, p3, w_own, w_other, y0, y1, y2, y3, kept):
    rows = p0.shape[0]
    depth = p0.shape[1]
    step = pl.program_id(0)
    half = pl.num_programs(0) // 2

    @pl.when(step == 0)
    def _():
        for index, piece in enumerate((p0, p1, p2, p3)):
            start = pl.multiple_of(lax.rem(place[0] + index, RING) * rows, rows)
            kept[pl.ds(start, rows), :] = piece[...]

    def finish(weight):
        total = dot(kept[...], weight[...], transposed).astype(BF16)
        for index, out in enumerate((y0, y1, y2, y3)):
            out[...] = total[index * rows : (index + 1) * rows, :]

    @pl.when(step < half)
    def _():
        finish(w_own)

    @pl.when(step >= half)
    def _():
        finish(w_other)


def project_down(place, pieces, w_own, w_other, transposed):
    rows, depth = pieces[0].shape
    columns = w_own.shape[0 if transposed else 1]
    tile = min(TILE, columns)
    half = columns // tile
    whole = pl.BlockSpec((rows, depth), lambda n: (0, 0))
    if transposed:
        own = pl.BlockSpec((tile, depth), lambda n: (jnp.minimum(n, half - 1), 0))
        other = pl.BlockSpec((tile, depth), lambda n: (jnp.maximum(n - half, 0), 0))
    else:
        own = pl.BlockSpec((depth, tile), lambda n: (0, jnp.minimum(n, half - 1)))
        other = pl.BlockSpec((depth, tile), lambda n: (0, jnp.maximum(n - half, 0)))
    outs = pl.pallas_call(
        functools.partial(down_kernel, transposed),
        grid=(2 * half,),
        in_specs=[pl.BlockSpec(memory_space=pltpu.SMEM)] + [whole] * RING + [own, other],
        out_specs=[pl.BlockSpec((rows, tile), lambda n: (0, n))] * RING
        + [pl.BlockSpec((RING * rows, depth), lambda n: (0, 0))],
        out_shape=[jax.ShapeDtypeStruct((rows, 2 * columns), BF16)] * RING
        + [jax.ShapeDtypeStruct((RING * rows, depth), BF16)],
        compiler_params=pltpu.CompilerParams(vmem_limit_bytes=LIMIT),
        cost_estimate=cost(
            RING * rows, depth, 2 * columns, 2 * (2 * depth * columns + 2 * RING * rows * (depth + columns))
        ),
    )(place, *pieces, w_own, w_other)
    return outs[:RING], outs[RING]


def weight_kernel(l_own, l_other, r_own, r_other, out):
    dims = (((0,), (0,)), ((), ()))
    total = lax.dot_general(l_own[...], r_own[...], dims, preferred_element_type=F32)
    total = total + lax.dot_general(l_other[...], r_other[...], dims, preferred_element_type=F32)
    out[...] = total.astype(BF16)


def weight_grad(l_own, l_other, r_own, r_other):
    tokens, rows = l_own.shape
    columns = r_own.shape[1]
    tile = min(TILE, rows)
    left = pl.BlockSpec((tokens, tile), lambda m: (0, m))
    right = pl.BlockSpec((tokens, columns), lambda m: (0, 0))
    return pl.pallas_call(
        weight_kernel,
        grid=(rows // tile,),
        in_specs=[left, left, right, right],
        out_specs=pl.BlockSpec((tile, columns), lambda m: (m, 0)),
        out_shape=jax.ShapeDtypeStruct((rows, columns), BF16),
        compiler_params=pltpu.CompilerParams(vmem_limit_bytes=LIMIT),
        cost_estimate=cost(rows, 2 * tokens, columns, 2 * (rows * columns + 2 * tokens * (rows + columns))),
    )(l_own, l_other, r_own, r_other)


def gather_tokens(block):
    return gather_ring(jnp.concatenate(gather_ring(block, "first"), axis=0), "second")


def scatter_features(pieces):
    total = scatter_ring(pieces, "second")
    rows = total.shape[0] // RING
    blocks = [total[i * rows : (i + 1) * rows].astype(BF16) for i in range(RING)]
    return scatter_ring(blocks, "first").astype(BF16)


def local(inputs, w_in, w_out, cotangent):
    row = lax.axis_index("row")
    core = lax.rem(row, 2)
    place = jnp.reshape(lax.div(row, 2), (1,)).astype(jnp.int32)
    half, width = inputs.shape[0] // 2, inputs.shape[1]

    both = jnp.stack([inputs, cotangent]).reshape(2, 2, half, width)
    mine = lax.dynamic_index_in_dim(both, core, 1, keepdims=False)
    theirs = lax.dynamic_index_in_dim(both, 1 - core, 1, keepdims=False)
    chip = jnp.concatenate([mine, swap(theirs)], axis=2)
    w_in_other = swap(w_in)
    w_out_other = swap(w_out)

    input_pieces = gather_tokens(chip[0])
    cotangent_pieces = gather_tokens(chip[1])

    hidden_parts, input_own, input_sent = project_up(place, input_pieces, w_in, w_in_other, False)
    hidden = scatter_ring(hidden_parts, "up")
    grad_parts, cotangent_own, cotangent_sent = project_up(place, cotangent_pieces, w_out, w_out_other, True)

    activated = gather_ring(gelu_form(hidden).astype(BF16), "up")
    grad_activated = scatter_ring(grad_parts, "up")

    output_parts, activated_own = project_down(place, activated, w_out, w_out_other, False)
    grad_hidden = gather_ring(gelu_backward(hidden, grad_activated).astype(BF16), "up")
    output_half = scatter_features(output_parts)

    input_parts, grad_hidden_own = project_down(place, grad_hidden, w_in, w_in_other, True)
    grad_inputs_half = scatter_features(input_parts)

    grad_w_out = weight_grad(activated_own, swap(activated_own), cotangent_own, swap(cotangent_sent))
    grad_w_in = weight_grad(input_own, swap(input_sent), grad_hidden_own, swap(grad_hidden_own))

    def whole(part):
        kept, got = part[:, :width], swap(part[:, width:])
        return jnp.where(core == 0, jnp.concatenate([kept, got]), jnp.concatenate([got, kept]))

    return (whole(output_half), whole(grad_inputs_half), grad_w_in, grad_w_out)


def solution(mesh):
    in_specs = (P("col", "row"), P("row", "col"), P("col", "row"), P("col", "row"))
    out_specs = (P("col", "row"), P("col", "row"), P("row", "col"), P("col", "row"))
    return jax.shard_map(local, mesh=mesh, in_specs=in_specs, out_specs=out_specs, check_vma=False)
```

```python
import functools

import jax
import jax.numpy as jnp
from jax import lax
from jax.experimental import pallas as pl
from jax.experimental.pallas import tpu as pltpu
from jax.sharding import PartitionSpec as P

BF16 = jnp.bfloat16
F32 = jnp.float32
AXES = ("row", "col")
FAR = (1, 3)
NEAR = (3, 1)
RING = 4
TILE = 512
LIMIT = 62 * 1024 * 1024
SMALL = 16 * 1024 * 1024
ANYWHERE = pl.BlockSpec(memory_space=pl.ANY)


def gelu_form(value):
    return jax.nn.gelu(value, approximate=True)


def gelu_backward(value, grad):
    return jax.vjp(gelu_form, value)[1](grad)[0]


def permutation(first=0, second=0, other=0, flip=(0, 0)):
    pairs = []
    for z in range(RING):
        for core in range(2):
            for x in range(RING):
                for y in range(RING):
                    step_x, step_y = (first, second) if core == 0 else (second, first)
                    to_row = (z ^ flip[core]) * 2 + (core + other) % 2
                    to_col = ((x + step_x) % RING) * RING + (y + step_y) % RING
                    pairs.append(((z * 2 + core) * 16 + x * RING + y, to_row * 16 + to_col))
    return pairs


def send(block, **where):
    return lax.ppermute(block, AXES, permutation(**where))


def swap(block):
    return send(block, other=1)


def gather_ring(block, axis):
    return [block] + [send(block, **{axis: -step}) for step in range(1, RING)]


def scatter_ring(blocks, axis):
    got = [send(blocks[step], **{axis: step}) for step in range(1, RING)]
    total = blocks[0].astype(F32)
    for block in got:
        total = total + block.astype(F32)
    return total


def cost(rows, depth, columns, moved):
    return pl.CostEstimate(flops=2 * rows * depth * columns, bytes_accessed=moved, transcendentals=0)


def dot(left, right, transposed):
    return lax.dot_general(left, right, (((1,), (1 if transposed else 0,)), ((), ())), preferred_element_type=F32)


def up_kernel(transposed, place, p0, p1, p2, p3, w_own, w_other, after, keep, give, own, other, scratch):
    rows = p0.shape[0]
    depth = own.shape[1]

    @pl.when(pl.program_id(0) == 0)
    def _():
        start = 0
        for piece in (p0, p1, p2, p3):
            stop = start + piece.shape[0]
            own[start:stop, :] = piece[:, :depth]
            other[start:stop, :] = piece[:, depth:]
            start = stop

    total = dot(own[...], w_own[...], transposed) + dot(other[...], w_other[...], transposed)
    scratch[...] = total
    for index in range(RING):
        part = scratch[pl.ds(pl.multiple_of(place[index] * rows, rows), rows), :]
        if index < 2:
            keep[index * rows : (index + 1) * rows, :] = part
        else:
            give[(index - 2) * rows : (index - 1) * rows, :] = part.astype(BF16)


def project_up(place, pieces, w_own, w_other, transposed, after):
    rows, width = pieces[0].shape
    depth = width // 2
    columns = w_own.shape[0 if transposed else 1]
    tile = min(TILE, columns)
    whole = [pl.BlockSpec(piece.shape, lambda n: (0, 0)) for piece in pieces]
    if transposed:
        weight = pl.BlockSpec((tile, depth), lambda n: (n, 0))
    else:
        weight = pl.BlockSpec((depth, tile), lambda n: (0, n))
    kept = pl.BlockSpec((RING * rows, depth), lambda n: (0, 0))
    outs = pl.pallas_call(
        functools.partial(up_kernel, transposed),
        grid=(columns // tile,),
        in_specs=[pl.BlockSpec(memory_space=pltpu.SMEM)] + whole + [weight] * 2 + [ANYWHERE],
        out_specs=[pl.BlockSpec((2 * rows, tile), lambda n: (0, n))] * 2 + [kept] * 2,
        out_shape=[jax.ShapeDtypeStruct((2 * rows, columns), dtype) for dtype in (F32, BF16)]
        + [jax.ShapeDtypeStruct((RING * rows, depth), BF16)] * 2,
        scratch_shapes=[pltpu.VMEM((RING * rows, tile), F32)],
        compiler_params=pltpu.CompilerParams(vmem_limit_bytes=LIMIT),
        cost_estimate=cost(RING * rows, width, columns, 2 * (width * columns + 2 * RING * rows * width)),
    )(place, *pieces, w_own, w_other, after)
    return outs


def down_kernel(transposed, place, near, far, w_own, w_other, after, later, y0, y1, y2, y3, kept):
    rows = near.shape[0] // 2
    step = pl.program_id(0)
    half = pl.num_programs(0) // 2

    @pl.when(step == 0)
    def _():
        for index in range(RING):
            piece = (near, far)[index // 2]
            start = pl.multiple_of(place[index] * rows, rows)
            kept[pl.ds(start, rows), :] = piece[(index % 2) * rows : (index % 2 + 1) * rows, :]

    def finish(weight):
        total = dot(kept[...], weight[...], transposed).astype(BF16)
        for index, out in enumerate((y0, y1, y2, y3)):
            out[...] = total[index * rows : (index + 1) * rows, :]

    @pl.when(step < half)
    def _():
        finish(w_own)

    @pl.when(step >= half)
    def _():
        finish(w_other)


def project_down(place, pieces, w_own, w_other, transposed, after):
    rows, depth = pieces[0].shape[0] // 2, pieces[0].shape[1]
    columns = w_own.shape[0 if transposed else 1]
    tile = min(TILE, columns)
    half = columns // tile
    whole = pl.BlockSpec((2 * rows, depth), lambda n: (0, 0))
    if transposed:
        own = pl.BlockSpec((tile, depth), lambda n: (jnp.minimum(n, half - 1), 0))
        other = pl.BlockSpec((tile, depth), lambda n: (jnp.maximum(n - half, 0), 0))
    else:
        own = pl.BlockSpec((depth, tile), lambda n: (0, jnp.minimum(n, half - 1)))
        other = pl.BlockSpec((depth, tile), lambda n: (0, jnp.maximum(n - half, 0)))
    outs = pl.pallas_call(
        functools.partial(down_kernel, transposed),
        grid=(2 * half,),
        in_specs=[pl.BlockSpec(memory_space=pltpu.SMEM)] + [whole] * 2 + [own, other, ANYWHERE, ANYWHERE],
        out_specs=[pl.BlockSpec((rows, tile), lambda n: (0, n))] * RING
        + [pl.BlockSpec((RING * rows, depth), lambda n: (0, 0))],
        out_shape=[jax.ShapeDtypeStruct((rows, 2 * columns), BF16)] * RING
        + [jax.ShapeDtypeStruct((RING * rows, depth), BF16)],
        compiler_params=pltpu.CompilerParams(vmem_limit_bytes=LIMIT),
        cost_estimate=cost(
            RING * rows, depth, 2 * columns, 2 * (2 * depth * columns + 2 * RING * rows * (depth + columns))
        ),
    )(place, *pieces, w_own, w_other, *after)
    return outs[:RING], outs[RING]


def weight_kernel(l_own, l_other, r_own, r_other, after, out):
    dims = (((0,), (0,)), ((), ()))
    total = lax.dot_general(l_own[...], r_own[...], dims, preferred_element_type=F32)
    total = total + lax.dot_general(l_other[...], r_other[...], dims, preferred_element_type=F32)
    out[...] = total.astype(BF16)


def weight_grad(l_own, l_other, r_own, r_other, after):
    tokens, rows = l_own.shape
    columns = r_own.shape[1]
    tile = min(TILE, rows)
    left = pl.BlockSpec((tokens, tile), lambda m: (0, m))
    right = pl.BlockSpec((tokens, columns), lambda m: (0, 0))
    return pl.pallas_call(
        weight_kernel,
        grid=(rows // tile,),
        in_specs=[left, left, right, right, ANYWHERE],
        out_specs=pl.BlockSpec((tile, columns), lambda m: (m, 0)),
        out_shape=jax.ShapeDtypeStruct((rows, columns), BF16),
        compiler_params=pltpu.CompilerParams(vmem_limit_bytes=LIMIT),
        cost_estimate=cost(rows, 2 * tokens, columns, 2 * (rows * columns + 2 * tokens * (rows + columns))),
    )(l_own, l_other, r_own, r_other, after)


def join_kernel(p0, p1, p2, p3, after, out):
    rows = p0.shape[0] // 2
    for index, piece in enumerate((p0, p1, p2, p3)):
        out[index * rows : (index + 1) * rows, :] = piece[rows:, :]


def join(parts, after):
    rows, width = parts[0].shape
    whole = pl.BlockSpec(memory_space=pltpu.VMEM)
    return pl.pallas_call(
        join_kernel,
        in_specs=[whole] * RING + [ANYWHERE],
        out_specs=whole,
        out_shape=jax.ShapeDtypeStruct((2 * rows, width), BF16),
        compiler_params=pltpu.CompilerParams(vmem_limit_bytes=SMALL),
        cost_estimate=cost(0, 0, 0, 4 * rows * width),
    )(*parts, after)


def add_kernel(p0, p1, p2, p3, first, z0, z1, z2, z3):
    total = p0[...].astype(F32) + p1[...].astype(F32) + p2[...].astype(F32) + p3[...].astype(F32)
    total = total.astype(BF16)
    rows = z0.shape[0] // 2
    for index, out in enumerate((z0, z1, z2, z3)):
        out[:rows, :] = first[index * rows : (index + 1) * rows, :]
        out[rows:, :] = total[index * rows : (index + 1) * rows, :]


def add_parts(parts, first):
    rows, width = parts[0].shape
    tile = min(1024, width)
    return pl.pallas_call(
        add_kernel,
        grid=(width // tile,),
        in_specs=[pl.BlockSpec((rows, tile), lambda n: (0, n))] * (RING + 1),
        out_specs=[pl.BlockSpec((rows // 2, tile), lambda n: (0, n))] * RING,
        out_shape=[jax.ShapeDtypeStruct((rows // 2, width), BF16)] * RING,
        compiler_params=pltpu.CompilerParams(vmem_limit_bytes=SMALL),
        cost_estimate=cost(0, 0, 0, 4 * rows * width),
    )(*parts, first)


def together(*values):
    return lax.optimization_barrier(values)


def total_of(blocks):
    total = blocks[0].astype(F32)
    for block in blocks[1:]:
        total = total + block.astype(F32)
    return total


def scatter_far(keep, got):
    rows = keep.shape[0] // 2
    total = keep + got.astype(F32)
    return lax.optimization_barrier((total[:rows], total[rows:].astype(BF16)))


def gather_near(block):
    return jnp.concatenate([block, send(block, flip=NEAR)])


def exchange(blocks, axis):
    return [blocks[0]] + [send(blocks[step], **{axis: step}) for step in range(1, RING)]


def local(inputs, w_in, w_out, cotangent):
    row = lax.axis_index("row")
    core = lax.rem(row, 2)
    level = lax.div(row, 2)
    far = jnp.where(core == 0, FAR[0], FAR[1])
    place = jnp.stack([level, level ^ far ^ 2, level ^ far, level ^ 2]).astype(jnp.int32)
    half, width = inputs.shape[0] // 2, inputs.shape[1]

    def halves(which):
        return [lax.dynamic_slice_in_dim(block, which * half, half) for block in (inputs, cotangent)]

    chip = jnp.concatenate([jnp.concatenate(halves(core)), swap(jnp.concatenate(halves(1 - core)))], axis=1)
    w_in_late, chip = together(w_in, chip)
    w_in_other = swap(w_in_late)

    parts = gather_ring(chip, "first")
    input_block, w_out_late, w_in_other = together(
        jnp.concatenate([part[:half] for part in parts]), w_out, w_in_other
    )
    w_out_other = swap(w_out_late)
    input_pieces = gather_ring(input_block, "second")
    cotangent_block, w_out_other = together(join(parts, input_pieces[1]), w_out_other)
    cotangent_pieces = gather_ring(cotangent_block, "second")

    keep, give, input_own, input_sent = project_up(place, input_pieces, w_in, w_in_other, False, cotangent_block)
    give, cotangent_pieces[1], cotangent_pieces[3] = together(give, cotangent_pieces[1], cotangent_pieces[3])
    hidden, passed = scatter_far(keep, send(give, flip=FAR))
    passed, input_got = together(passed, swap(input_sent))
    hidden_got = send(passed, flip=NEAR)
    keep, give, cotangent_own, cotangent_sent = project_up(
        place, cotangent_pieces, w_out, w_out_other, True, passed
    )
    give, hidden_got = together(give, hidden_got)

    hidden = hidden + hidden_got.astype(F32)
    hidden, activated = together(hidden, gelu_form(hidden).astype(BF16))
    grad_got, near = together(send(give, flip=FAR), gather_near(activated))
    activated = [near, send(near, flip=FAR)]
    grad_activated, passed = scatter_far(keep, grad_got)
    passed, cotangent_got = together(passed, swap(cotangent_sent))

    grad_activated = grad_activated + send(passed, flip=NEAR).astype(F32)
    grad_hidden = gelu_backward(hidden, grad_activated).astype(BF16)
    near = gather_near(grad_hidden)
    grad_hidden = [near, send(near, flip=FAR)]
    output_parts, activated_own = project_down(
        place, activated, w_out, w_out_other, False, (near, input_got)
    )
    activated_got = swap(activated_own)
    output_blocks = exchange(output_parts, "second")

    input_parts, grad_hidden_own = project_down(
        place, grad_hidden, w_in, w_in_other, True, (activated_own, place)
    )
    input_blocks = exchange(input_parts, "second")
    output_sum = total_of(output_blocks).astype(BF16)
    grad_w_out = weight_grad(activated_own, activated_got, cotangent_own, cotangent_got, output_sum)
    grad_w_in = weight_grad(input_own, input_got, grad_hidden_own, swap(grad_hidden_own), grad_w_out)
    *input_blocks, output_sum, grad_w_in = together(*input_blocks, output_sum, grad_w_in)
    both = scatter_ring(add_parts(input_blocks, output_sum), "first").astype(BF16)
    kept, got = both[:, :width], swap(both[:, width:])

    def whole(start):
        mine, theirs = kept[start : start + half], got[start : start + half]
        return jnp.where(core == 0, jnp.concatenate([mine, theirs]), jnp.concatenate([theirs, mine]))

    return (whole(0), whole(half), grad_w_in, grad_w_out)


def solution(mesh):
    in_specs = (P("col", "row"), P("row", "col"), P("col", "row"), P("col", "row"))
    out_specs = (P("col", "row"), P("col", "row"), P("row", "col"), P("col", "row"))
    return jax.shard_map(local, mesh=mesh, in_specs=in_specs, out_specs=out_specs, check_vma=False)
```

```python
import functools

import jax
import jax.numpy as jnp
from jax import lax
from jax.experimental import pallas as pl
from jax.experimental.pallas import tpu as pltpu
from jax.sharding import PartitionSpec as P

BF16 = jnp.bfloat16
F32 = jnp.float32
AXES = ("row", "col")
FAR = (1, 3)
NEAR = (3, 1)
RING = 4
TILE = 512
LIMIT = 30 * 1024 * 1024
SMALL = 16 * 1024 * 1024
ANYWHERE = pl.BlockSpec(memory_space=pl.ANY)


def gelu_form(value):
    return jax.nn.gelu(value, approximate=True)


def gelu_backward(value, grad):
    return jax.vjp(gelu_form, value)[1](grad)[0]


def permutation(first=0, second=0, other=0, flip=(0, 0)):
    pairs = []
    for z in range(RING):
        for core in range(2):
            for x in range(RING):
                for y in range(RING):
                    step_x, step_y = (first, second) if core == 0 else (second, first)
                    to_row = (z ^ flip[core]) * 2 + (core + other) % 2
                    to_col = ((x + step_x) % RING) * RING + (y + step_y) % RING
                    pairs.append(((z * 2 + core) * 16 + x * RING + y, to_row * 16 + to_col))
    return pairs


def send(block, **where):
    return lax.ppermute(block, AXES, permutation(**where))


def swap(block):
    return send(block, other=1)


def gather_ring(block, axis):
    return [block] + [send(block, **{axis: -step}) for step in range(1, RING)]


def scatter_ring(blocks, axis):
    got = [send(blocks[step], **{axis: step}) for step in range(1, RING)]
    total = blocks[0].astype(F32)
    for block in got:
        total = total + block.astype(F32)
    return total


def cost(rows, depth, columns, moved):
    return pl.CostEstimate(flops=2 * rows * depth * columns, bytes_accessed=moved, transcendentals=0)


def dot(left, right, transposed):
    return lax.dot_general(left, right, (((1,), (1 if transposed else 0,)), ((), ())), preferred_element_type=F32)


def up_kernel(transposed, place, p0, p1, p2, p3, w_own, w_other, after, keep, give, own, other, scratch, tiles, sems):
    rows = p0.shape[0]
    depth = own.shape[1]
    step = pl.program_id(0)

    def fetch(index):
        width = scratch.shape[1]
        part = pl.ds(pl.multiple_of(index * width, width), width)
        source = w_own.at[part, :] if transposed else w_own.at[:, part]
        return pltpu.make_async_copy(source, tiles.at[index], sems.at[index])

    @pl.when(step == 0)
    def _():
        for index in range(tiles.shape[0]):
            fetch(index).start()
        start = 0
        for piece in (p0, p1, p2, p3):
            stop = start + piece.shape[0]
            own[start:stop, :] = piece[:, :depth]
            other[start:stop, :] = piece[:, depth:]
            start = stop

    total = dot(other[...], w_other[...], transposed)
    fetch(step).wait()
    scratch[...] = total + dot(own[...], tiles[step], transposed)
    for index in range(RING):
        part = scratch[pl.ds(pl.multiple_of(place[index] * rows, rows), rows), :]
        if index < 2:
            keep[index * rows : (index + 1) * rows, :] = part
        else:
            give[(index - 2) * rows : (index - 1) * rows, :] = part.astype(BF16)


def project_up(place, pieces, w_own, w_other, transposed, after):
    rows, width = pieces[0].shape
    depth = width // 2
    columns = w_own.shape[0 if transposed else 1]
    tile = min(TILE, columns)
    whole = [pl.BlockSpec(piece.shape, lambda n: (0, 0)) for piece in pieces]
    if transposed:
        weight = pl.BlockSpec((tile, depth), lambda n: (n, 0))
    else:
        weight = pl.BlockSpec((depth, tile), lambda n: (0, n))
    kept = pl.BlockSpec((RING * rows, depth), lambda n: (0, 0))
    outs = pl.pallas_call(
        functools.partial(up_kernel, transposed),
        grid=(columns // tile,),
        in_specs=[pl.BlockSpec(memory_space=pltpu.SMEM)] + whole + [pl.BlockSpec(memory_space=pltpu.HBM), weight, ANYWHERE],
        out_specs=[pl.BlockSpec((2 * rows, tile), lambda n: (0, n))] * 2 + [kept] * 2,
        out_shape=[jax.ShapeDtypeStruct((2 * rows, columns), dtype) for dtype in (F32, BF16)]
        + [jax.ShapeDtypeStruct((RING * rows, depth), BF16)] * 2,
        scratch_shapes=[
            pltpu.VMEM((RING * rows, tile), F32),
            pltpu.VMEM((columns // tile, tile, depth) if transposed else (columns // tile, depth, tile), BF16),
            pltpu.SemaphoreType.DMA((columns // tile,)),
        ],
        compiler_params=pltpu.CompilerParams(vmem_limit_bytes=LIMIT),
        cost_estimate=cost(RING * rows, width, columns, 2 * (width * columns + 2 * RING * rows * width)),
    )(place, *pieces, w_own, w_other, after)
    return outs


def down_kernel(transposed, place, near, far, w_own, w_other, after, later, y0, y1, y2, y3, kept):
    rows = near.shape[0] // 2
    step = pl.program_id(0)
    half = pl.num_programs(0) // 2

    @pl.when(step == 0)
    def _():
        for index in range(RING):
            piece = (near, far)[index // 2]
            start = pl.multiple_of(place[index] * rows, rows)
            kept[pl.ds(start, rows), :] = piece[(index % 2) * rows : (index % 2 + 1) * rows, :]

    def finish(weight):
        total = dot(kept[...], weight[...], transposed).astype(BF16)
        for index, out in enumerate((y0, y1, y2, y3)):
            out[...] = total[index * rows : (index + 1) * rows, :]

    @pl.when(step < half)
    def _():
        finish(w_own)

    @pl.when(step >= half)
    def _():
        finish(w_other)


def project_down(place, pieces, w_own, w_other, transposed, after):
    rows, depth = pieces[0].shape[0] // 2, pieces[0].shape[1]
    columns = w_own.shape[0 if transposed else 1]
    tile = min(TILE, columns)
    half = columns // tile
    whole = pl.BlockSpec((2 * rows, depth), lambda n: (0, 0))
    if transposed:
        own = pl.BlockSpec((tile, depth), lambda n: (jnp.minimum(n, half - 1), 0))
        other = pl.BlockSpec((tile, depth), lambda n: (jnp.maximum(n - half, 0), 0))
    else:
        own = pl.BlockSpec((depth, tile), lambda n: (0, jnp.minimum(n, half - 1)))
        other = pl.BlockSpec((depth, tile), lambda n: (0, jnp.maximum(n - half, 0)))
    outs = pl.pallas_call(
        functools.partial(down_kernel, transposed),
        grid=(2 * half,),
        in_specs=[pl.BlockSpec(memory_space=pltpu.SMEM)] + [whole] * 2 + [own, other, ANYWHERE, ANYWHERE],
        out_specs=[pl.BlockSpec((rows, tile), lambda n: (0, n))] * RING
        + [pl.BlockSpec((RING * rows, depth), lambda n: (0, 0))],
        out_shape=[jax.ShapeDtypeStruct((rows, 2 * columns), BF16)] * RING
        + [jax.ShapeDtypeStruct((RING * rows, depth), BF16)],
        compiler_params=pltpu.CompilerParams(vmem_limit_bytes=LIMIT),
        cost_estimate=cost(
            RING * rows, depth, 2 * columns, 2 * (2 * depth * columns + 2 * RING * rows * (depth + columns))
        ),
    )(place, *pieces, w_own, w_other, *after)
    return outs[:RING], outs[RING]


def weight_kernel(l_own, l_other, r_own, r_other, after, out):
    dims = (((0,), (0,)), ((), ()))
    total = lax.dot_general(l_own[...], r_own[...], dims, preferred_element_type=F32)
    total = total + lax.dot_general(l_other[...], r_other[...], dims, preferred_element_type=F32)
    out[...] = total.astype(BF16)


def weight_grad(l_own, l_other, r_own, r_other, after):
    tokens, rows = l_own.shape
    columns = r_own.shape[1]
    tile = min(TILE, rows)
    left = pl.BlockSpec((tokens, tile), lambda m: (0, m))
    right = pl.BlockSpec((tokens, columns), lambda m: (0, 0))
    return pl.pallas_call(
        weight_kernel,
        grid=(rows // tile,),
        in_specs=[left, left, right, right, ANYWHERE],
        out_specs=pl.BlockSpec((tile, columns), lambda m: (m, 0)),
        out_shape=jax.ShapeDtypeStruct((rows, columns), BF16),
        compiler_params=pltpu.CompilerParams(vmem_limit_bytes=LIMIT),
        cost_estimate=cost(rows, 2 * tokens, columns, 2 * (rows * columns + 2 * tokens * (rows + columns))),
    )(l_own, l_other, r_own, r_other, after)


def join_kernel(p0, p1, p2, p3, after, out):
    rows = p0.shape[0] // 2
    for index, piece in enumerate((p0, p1, p2, p3)):
        out[index * rows : (index + 1) * rows, :] = piece[rows:, :]


def join(parts, after):
    rows, width = parts[0].shape
    whole = pl.BlockSpec(memory_space=pltpu.VMEM)
    return pl.pallas_call(
        join_kernel,
        in_specs=[whole] * RING + [ANYWHERE],
        out_specs=whole,
        out_shape=jax.ShapeDtypeStruct((2 * rows, width), BF16),
        compiler_params=pltpu.CompilerParams(vmem_limit_bytes=SMALL),
        cost_estimate=cost(0, 0, 0, 4 * rows * width),
    )(*parts, after)


def add_kernel(p0, p1, p2, p3, first, z0, z1, z2, z3):
    total = p0[...].astype(F32) + p1[...].astype(F32) + p2[...].astype(F32) + p3[...].astype(F32)
    total = total.astype(BF16)
    rows = z0.shape[0] // 2
    for index, out in enumerate((z0, z1, z2, z3)):
        out[:rows, :] = first[index * rows : (index + 1) * rows, :]
        out[rows:, :] = total[index * rows : (index + 1) * rows, :]


def add_parts(parts, first):
    rows, width = parts[0].shape
    tile = min(1024, width)
    return pl.pallas_call(
        add_kernel,
        grid=(width // tile,),
        in_specs=[pl.BlockSpec((rows, tile), lambda n: (0, n))] * (RING + 1),
        out_specs=[pl.BlockSpec((rows // 2, tile), lambda n: (0, n))] * RING,
        out_shape=[jax.ShapeDtypeStruct((rows // 2, width), BF16)] * RING,
        compiler_params=pltpu.CompilerParams(vmem_limit_bytes=SMALL),
        cost_estimate=cost(0, 0, 0, 4 * rows * width),
    )(*parts, first)


def together(*values):
    return lax.optimization_barrier(values)


def total_of(blocks):
    total = blocks[0].astype(F32)
    for block in blocks[1:]:
        total = total + block.astype(F32)
    return total


def scatter_far(keep, got):
    rows = keep.shape[0] // 2
    total = keep + got.astype(F32)
    return lax.optimization_barrier((total[:rows], total[rows:].astype(BF16)))


def gather_near(block):
    return jnp.concatenate([block, send(block, flip=NEAR)])


def exchange(blocks, axis):
    return [blocks[0]] + [send(blocks[step], **{axis: step}) for step in range(1, RING)]


def local(inputs, w_in, w_out, cotangent):
    row = lax.axis_index("row")
    core = lax.rem(row, 2)
    level = lax.div(row, 2)
    far = jnp.where(core == 0, FAR[0], FAR[1])
    place = jnp.stack([level, level ^ far ^ 2, level ^ far, level ^ 2]).astype(jnp.int32)
    half, width = inputs.shape[0] // 2, inputs.shape[1]

    def halves(which):
        return [lax.dynamic_slice_in_dim(block, which * half, half) for block in (inputs, cotangent)]

    chip = jnp.concatenate([jnp.concatenate(halves(core)), swap(jnp.concatenate(halves(1 - core)))], axis=1)
    w_in_late, chip = together(w_in, chip)
    w_in_other = swap(w_in_late)

    parts = gather_ring(chip, "first")
    input_block, w_out_late = together(jnp.concatenate([part[:half] for part in parts]), w_out)
    w_out_other = swap(w_out_late)
    input_pieces = gather_ring(input_block, "second")
    cotangent_block = join(parts, input_pieces[1])
    cotangent_pieces = gather_ring(cotangent_block, "second")

    keep, give, input_own, input_sent = project_up(place, input_pieces, w_in, w_in_other, False, cotangent_block)
    give, cotangent_pieces[1], cotangent_pieces[3] = together(give, cotangent_pieces[1], cotangent_pieces[3])
    hidden, passed = scatter_far(keep, send(give, flip=FAR))
    passed, input_got = together(passed, swap(input_sent))
    hidden_got = send(passed, flip=NEAR)
    keep, give, cotangent_own, cotangent_sent = project_up(
        place, cotangent_pieces, w_out, w_out_other, True, passed
    )
    give, hidden_got = together(give, hidden_got)

    hidden = hidden + hidden_got.astype(F32)
    hidden, activated = together(hidden, gelu_form(hidden).astype(BF16))
    grad_got, near = together(send(give, flip=FAR), gather_near(activated))
    activated = [near, send(near, flip=FAR)]
    grad_activated, passed = scatter_far(keep, grad_got)
    passed, cotangent_got = together(passed, swap(cotangent_sent))

    grad_activated = grad_activated + send(passed, flip=NEAR).astype(F32)
    grad_hidden = gelu_backward(hidden, grad_activated).astype(BF16)
    near = gather_near(grad_hidden)
    grad_hidden = [near, send(near, flip=FAR)]
    output_parts, activated_own = project_down(
        place, activated, w_out, w_out_other, False, (near, input_got)
    )
    activated_got = swap(activated_own)
    output_blocks = exchange(output_parts, "second")

    input_parts, grad_hidden_own = project_down(
        place, grad_hidden, w_in, w_in_other, True, (activated_own, place)
    )
    input_blocks = exchange(input_parts, "second")
    output_sum = total_of(output_blocks).astype(BF16)
    grad_w_out = weight_grad(activated_own, activated_got, cotangent_own, cotangent_got, output_sum)
    grad_hidden_got, grad_w_out = together(swap(grad_hidden_own), grad_w_out)
    grad_w_in = weight_grad(input_own, input_got, grad_hidden_own, grad_hidden_got, place)
    *input_blocks, output_sum, grad_w_in = together(*input_blocks, output_sum, grad_w_in)
    both = scatter_ring(add_parts(input_blocks, output_sum), "first").astype(BF16)
    kept, got = both[:, :width], swap(both[:, width:])

    def whole(start):
        mine, theirs = kept[start : start + half], got[start : start + half]
        return jnp.where(core == 0, jnp.concatenate([mine, theirs]), jnp.concatenate([theirs, mine]))

    return (whole(0), whole(half), grad_w_in, grad_w_out)


def solution(mesh):
    in_specs = (P("col", "row"), P("row", "col"), P("col", "row"), P("col", "row"))
    out_specs = (P("col", "row"), P("col", "row"), P("row", "col"), P("col", "row"))
    return jax.shard_map(local, mesh=mesh, in_specs=in_specs, out_specs=out_specs, check_vma=False)
```

```python
import functools

import jax
import jax.numpy as jnp
from jax import lax
from jax.experimental import pallas as pl
from jax.experimental.pallas import tpu as pltpu
from jax.sharding import PartitionSpec as P

BF16 = jnp.bfloat16
F32 = jnp.float32
AXES = ("row", "col")
FAR = (1, 3)
NEAR = (3, 1)
RING = 4
TILE = 512
LIMIT = 30 * 1024 * 1024
SMALL = 16 * 1024 * 1024
ANYWHERE = pl.BlockSpec(memory_space=pl.ANY)


def gelu_form(value):
    return jax.nn.gelu(value, approximate=True)


def gelu_backward(value, grad):
    return jax.vjp(gelu_form, value)[1](grad)[0]


def permutation(first=0, second=0, other=0, flip=(0, 0)):
    pairs = []
    for z in range(RING):
        for core in range(2):
            for x in range(RING):
                for y in range(RING):
                    step_x, step_y = (first, second) if core == 0 else (second, first)
                    to_row = (z ^ flip[core]) * 2 + (core + other) % 2
                    to_col = ((x + step_x) % RING) * RING + (y + step_y) % RING
                    pairs.append(((z * 2 + core) * 16 + x * RING + y, to_row * 16 + to_col))
    return pairs


def send(block, **where):
    return lax.ppermute(block, AXES, permutation(**where))


def swap(block):
    return send(block, other=1)


def gather_ring(block, axis):
    return [block] + [send(block, **{axis: -step}) for step in range(1, RING)]


def scatter_ring(blocks, axis):
    got = [send(blocks[step], **{axis: step}) for step in range(1, RING)]
    total = blocks[0].astype(F32)
    for block in got:
        total = total + block.astype(F32)
    return total


def cost(rows, depth, columns, moved):
    return pl.CostEstimate(flops=2 * rows * depth * columns, bytes_accessed=moved, transcendentals=0)


def dot(left, right, transposed):
    return lax.dot_general(left, right, (((1,), (1 if transposed else 0,)), ((), ())), preferred_element_type=F32)


def up_kernel(transposed, place, p0, p1, p2, p3, w_own, w_other, after, keep, give, own, other, scratch, tiles, sems):
    rows = p0.shape[0]
    depth = own.shape[1]
    step = pl.program_id(0)

    def fetch(index):
        width = scratch.shape[1]
        part = pl.ds(pl.multiple_of(index * width, width), width)
        source = w_own.at[part, :] if transposed else w_own.at[:, part]
        return pltpu.make_async_copy(source, tiles.at[index], sems.at[index])

    @pl.when(step == 0)
    def _():
        for index in range(tiles.shape[0]):
            fetch(index).start()
        start = 0
        for piece in (p0, p1, p2, p3):
            stop = start + piece.shape[0]
            own[start:stop, :] = piece[:, :depth]
            other[start:stop, :] = piece[:, depth:]
            start = stop

    total = dot(other[...], w_other[...], transposed)
    fetch(step).wait()
    scratch[...] = total + dot(own[...], tiles[step], transposed)
    for index in range(RING):
        part = scratch[pl.ds(pl.multiple_of(place[index] * rows, rows), rows), :]
        if index < 2:
            keep[index * rows : (index + 1) * rows, :] = part
        else:
            give[(index - 2) * rows : (index - 1) * rows, :] = part.astype(BF16)


def project_up(place, pieces, w_own, w_other, transposed, after):
    rows, width = pieces[0].shape
    depth = width // 2
    columns = w_own.shape[0 if transposed else 1]
    tile = min(TILE, columns)
    whole = [pl.BlockSpec(piece.shape, lambda n: (0, 0)) for piece in pieces]
    if transposed:
        weight = pl.BlockSpec((tile, depth), lambda n: (n, 0))
    else:
        weight = pl.BlockSpec((depth, tile), lambda n: (0, n))
    kept = pl.BlockSpec((RING * rows, depth), lambda n: (0, 0))
    outs = pl.pallas_call(
        functools.partial(up_kernel, transposed),
        grid=(columns // tile,),
        in_specs=[pl.BlockSpec(memory_space=pltpu.SMEM)] + whole + [pl.BlockSpec(memory_space=pltpu.HBM), weight, ANYWHERE],
        out_specs=[pl.BlockSpec((2 * rows, tile), lambda n: (0, n))] * 2 + [kept] * 2,
        out_shape=[jax.ShapeDtypeStruct((2 * rows, columns), dtype) for dtype in (F32, BF16)]
        + [jax.ShapeDtypeStruct((RING * rows, depth), BF16)] * 2,
        scratch_shapes=[
            pltpu.VMEM((RING * rows, tile), F32),
            pltpu.VMEM((columns // tile, tile, depth) if transposed else (columns // tile, depth, tile), BF16),
            pltpu.SemaphoreType.DMA((columns // tile,)),
        ],
        compiler_params=pltpu.CompilerParams(vmem_limit_bytes=LIMIT),
        cost_estimate=cost(RING * rows, width, columns, 2 * (width * columns + 2 * RING * rows * width)),
    )(place, *pieces, w_own, w_other, after)
    return outs


def down_kernel(transposed, place, near, far, w_own, w_other, after, later, y0, y1, y2, y3, kept):
    rows = near.shape[0] // 2
    step = pl.program_id(0)
    half = pl.num_programs(0) // 2

    @pl.when(step == 0)
    def _():
        for index in range(RING):
            piece = (near, far)[index // 2]
            start = pl.multiple_of(place[index] * rows, rows)
            kept[pl.ds(start, rows), :] = piece[(index % 2) * rows : (index % 2 + 1) * rows, :]

    def finish(weight):
        total = dot(kept[...], weight[...], transposed).astype(BF16)
        for index, out in enumerate((y0, y1, y2, y3)):
            out[...] = total[index * rows : (index + 1) * rows, :]

    @pl.when(step < half)
    def _():
        finish(w_own)

    @pl.when(step >= half)
    def _():
        finish(w_other)


def project_down(place, pieces, w_own, w_other, transposed, after):
    rows, depth = pieces[0].shape[0] // 2, pieces[0].shape[1]
    columns = w_own.shape[0 if transposed else 1]
    tile = min(TILE, columns)
    half = columns // tile
    whole = pl.BlockSpec((2 * rows, depth), lambda n: (0, 0))
    if transposed:
        own = pl.BlockSpec((tile, depth), lambda n: (jnp.minimum(n, half - 1), 0))
        other = pl.BlockSpec((tile, depth), lambda n: (jnp.maximum(n - half, 0), 0))
    else:
        own = pl.BlockSpec((depth, tile), lambda n: (0, jnp.minimum(n, half - 1)))
        other = pl.BlockSpec((depth, tile), lambda n: (0, jnp.maximum(n - half, 0)))
    outs = pl.pallas_call(
        functools.partial(down_kernel, transposed),
        grid=(2 * half,),
        in_specs=[pl.BlockSpec(memory_space=pltpu.SMEM)] + [whole] * 2 + [own, other, ANYWHERE, ANYWHERE],
        out_specs=[pl.BlockSpec((rows, tile), lambda n: (0, n))] * RING
        + [pl.BlockSpec((RING * rows, depth), lambda n: (0, 0))],
        out_shape=[jax.ShapeDtypeStruct((rows, 2 * columns), BF16)] * RING
        + [jax.ShapeDtypeStruct((RING * rows, depth), BF16)],
        compiler_params=pltpu.CompilerParams(vmem_limit_bytes=LIMIT),
        cost_estimate=cost(
            RING * rows, depth, 2 * columns, 2 * (2 * depth * columns + 2 * RING * rows * (depth + columns))
        ),
    )(place, *pieces, w_own, w_other, *after)
    return outs[:RING], outs[RING]


def weight_kernel(l_own, l_other, r_own, r_other, after, out):
    dims = (((0,), (0,)), ((), ()))
    total = lax.dot_general(l_own[...], r_own[...], dims, preferred_element_type=F32)
    total = total + lax.dot_general(l_other[...], r_other[...], dims, preferred_element_type=F32)
    out[...] = total.astype(BF16)


def weight_grad(l_own, l_other, r_own, r_other, after):
    tokens, rows = l_own.shape
    columns = r_own.shape[1]
    tile = min(TILE, rows)
    left = pl.BlockSpec((tokens, tile), lambda m: (0, m))
    right = pl.BlockSpec((tokens, columns), lambda m: (0, 0))
    return pl.pallas_call(
        weight_kernel,
        grid=(rows // tile,),
        in_specs=[left, left, right, right, ANYWHERE],
        out_specs=pl.BlockSpec((tile, columns), lambda m: (m, 0)),
        out_shape=jax.ShapeDtypeStruct((rows, columns), BF16),
        compiler_params=pltpu.CompilerParams(vmem_limit_bytes=LIMIT),
        cost_estimate=cost(rows, 2 * tokens, columns, 2 * (rows * columns + 2 * tokens * (rows + columns))),
    )(l_own, l_other, r_own, r_other, after)


def join_kernel(p0, p1, p2, p3, after, out):
    rows = p0.shape[0] // 2
    for index, piece in enumerate((p0, p1, p2, p3)):
        out[index * rows : (index + 1) * rows, :] = piece[rows:, :]


def join(parts, after):
    rows, width = parts[0].shape
    whole = pl.BlockSpec(memory_space=pltpu.VMEM)
    return pl.pallas_call(
        join_kernel,
        in_specs=[whole] * RING + [ANYWHERE],
        out_specs=whole,
        out_shape=jax.ShapeDtypeStruct((2 * rows, width), BF16),
        compiler_params=pltpu.CompilerParams(vmem_limit_bytes=SMALL),
        cost_estimate=cost(0, 0, 0, 4 * rows * width),
    )(*parts, after)


def add_kernel(p0, p1, p2, p3, first, z0, z1, z2, z3):
    total = p0[...].astype(F32) + p1[...].astype(F32) + p2[...].astype(F32) + p3[...].astype(F32)
    total = total.astype(BF16)
    rows = z0.shape[0] // 2
    for index, out in enumerate((z0, z1, z2, z3)):
        out[:rows, :] = first[index * rows : (index + 1) * rows, :]
        out[rows:, :] = total[index * rows : (index + 1) * rows, :]


def add_parts(parts, first):
    rows, width = parts[0].shape
    tile = min(1024, width)
    return pl.pallas_call(
        add_kernel,
        grid=(width // tile,),
        in_specs=[pl.BlockSpec((rows, tile), lambda n: (0, n))] * (RING + 1),
        out_specs=[pl.BlockSpec((rows // 2, tile), lambda n: (0, n))] * RING,
        out_shape=[jax.ShapeDtypeStruct((rows // 2, width), BF16)] * RING,
        compiler_params=pltpu.CompilerParams(vmem_limit_bytes=SMALL),
        cost_estimate=cost(0, 0, 0, 4 * rows * width),
    )(*parts, first)


def together(*values):
    return lax.optimization_barrier(values)


def total_of(blocks):
    total = blocks[0].astype(F32)
    for block in blocks[1:]:
        total = total + block.astype(F32)
    return total


def scatter_far(keep, got):
    rows = keep.shape[0] // 2
    total = keep + got.astype(F32)
    return lax.optimization_barrier((total[:rows], total[rows:].astype(BF16)))


def gather_near(block):
    return jnp.concatenate([block, send(block, flip=NEAR)])


def exchange(blocks, axis):
    return [blocks[0]] + [send(blocks[step], **{axis: step}) for step in range(1, RING)]


def local(inputs, w_in, w_out, cotangent):
    row = lax.axis_index("row")
    core = lax.rem(row, 2)
    level = lax.div(row, 2)
    far = jnp.where(core == 0, FAR[0], FAR[1])
    place = jnp.stack([level, level ^ far ^ 2, level ^ far, level ^ 2]).astype(jnp.int32)
    half, width = inputs.shape[0] // 2, inputs.shape[1]

    def halves(blocks, which):
        return jnp.concatenate([lax.dynamic_slice_in_dim(block, which * half, half) for block in blocks])

    theirs, inputs, cotangent = together(halves((inputs, cotangent), 1 - core), inputs, cotangent)
    chip = jnp.concatenate([halves((inputs, cotangent), core), swap(theirs)], axis=1)
    w_in_late, chip = together(w_in, chip)
    w_in_other = swap(w_in_late)

    parts = gather_ring(chip, "first")
    input_block, w_out_late = together(jnp.concatenate([part[:half] for part in parts]), w_out)
    w_out_other = swap(w_out_late)
    input_pieces = gather_ring(input_block, "second")
    cotangent_block = join(parts, input_pieces[1])
    cotangent_pieces = gather_ring(cotangent_block, "second")

    keep, give, input_own, input_sent = project_up(place, input_pieces, w_in, w_in_other, False, cotangent_block)
    give, cotangent_pieces[1], cotangent_pieces[3] = together(give, cotangent_pieces[1], cotangent_pieces[3])
    hidden, passed = scatter_far(keep, send(give, flip=FAR))
    passed, input_got = together(passed, swap(input_sent))
    hidden_got = send(passed, flip=NEAR)
    keep, give, cotangent_own, cotangent_sent = project_up(
        place, cotangent_pieces, w_out, w_out_other, True, passed
    )
    give, hidden_got = together(give, hidden_got)

    hidden = hidden + hidden_got.astype(F32)
    hidden, activated = together(hidden, gelu_form(hidden).astype(BF16))
    grad_got, near = together(send(give, flip=FAR), gather_near(activated))
    activated = [near, send(near, flip=FAR)]
    grad_activated, passed = scatter_far(keep, grad_got)
    passed, cotangent_got = together(passed, swap(cotangent_sent))

    grad_activated = grad_activated + send(passed, flip=NEAR).astype(F32)
    grad_hidden = gelu_backward(hidden, grad_activated).astype(BF16)
    near = gather_near(grad_hidden)
    grad_hidden = [near, send(near, flip=FAR)]
    output_parts, activated_own = project_down(
        place, activated, w_out, w_out_other, False, (near, input_got)
    )
    activated_got = swap(activated_own)
    output_blocks = exchange(output_parts, "second")

    input_parts, grad_hidden_own = project_down(
        place, grad_hidden, w_in, w_in_other, True, (activated_own, place)
    )
    input_blocks = exchange(input_parts, "second")
    output_sum = total_of(output_blocks).astype(BF16)
    grad_w_out = weight_grad(activated_own, activated_got, cotangent_own, cotangent_got, output_sum)
    grad_hidden_got, grad_w_out = together(swap(grad_hidden_own), grad_w_out)
    grad_w_in = weight_grad(input_own, input_got, grad_hidden_own, grad_hidden_got, place)
    *input_blocks, output_sum, grad_w_in = together(*input_blocks, output_sum, grad_w_in)
    both = scatter_ring(add_parts(input_blocks, output_sum), "first").astype(BF16)
    kept, got = both[:, :width], swap(both[:, width:])

    def whole(start):
        mine, theirs = kept[start : start + half], got[start : start + half]
        return jnp.where(core == 0, jnp.concatenate([mine, theirs]), jnp.concatenate([theirs, mine]))

    return (whole(0), whole(half), grad_w_in, grad_w_out)


def solution(mesh):
    in_specs = (P("col", "row"), P("row", "col"), P("col", "row"), P("col", "row"))
    out_specs = (P("col", "row"), P("col", "row"), P("row", "col"), P("col", "row"))
    return jax.shard_map(local, mesh=mesh, in_specs=in_specs, out_specs=out_specs, check_vma=False)
```
